32 devices in a mesh: ctx: 16 (over z, y, x), wa: 2 (over core).
Axes of the slice: x: 2, y: 2, z: 4, core: 2. Of those that a mesh axis runs over, the one named last changes fastest.
Arguments:
- tokens: bfloat16 [4096, 768], P('ctx'), may hold values from -6 to 6
- cotangent: bfloat16 [4096, 768], P('ctx'), may hold values from -6 to 6
- routes: int32 [4096, 2], P('ctx'), may hold values from 0 to 15, all different within a row; in each aligned block of 256 rows (0 to 255, 256 to 511, ...) at most 64 rows name the same one
- buckets: int32 [1024], replicated, may hold values from 0 to 31
- block_order: int32 [16], replicated, may hold values from 0 to 15, each once
- attend_gain1: float32 [768], replicated, may hold values from 0.5 to 1.5
- rel_bias1: float32 [12, 32], P('wa'), may hold values from -4 to 4
- query_proj1: bfloat16 [768, 768], P('ctx', 'wa'), may hold values from -0.21875 to 0.21875
- key_proj1: bfloat16 [768, 768], P('ctx', 'wa'), may hold values from -0.21875 to 0.21875
- value_proj1: bfloat16 [768, 768], P('ctx', 'wa'), may hold values from -0.21875 to 0.21875
- output_proj1: bfloat16 [768, 768], P('ctx', 'wa'), may hold values from -0.625 to 0.625
- dense_gain1: float32 [768], replicated, may hold values from 0.5 to 1.5
- dense_up1: bfloat16 [768, 3072], P('ctx', 'wa'), may hold values from -0.21875 to 0.21875
- dense_down1: bfloat16 [768, 3072], P('ctx', 'wa'), may hold values from -0.109375 to 0.109375
- attend_gain2: float32 [768], replicated, may hold values from 0.5 to 1.5
- rel_bias2: float32 [12, 32], P('wa'), may hold values from -4 to 4
- query_proj2: bfloat16 [768, 768], P('ctx', 'wa'), may hold values from -0.21875 to 0.21875
- key_proj2: bfloat16 [768, 768], P('ctx', 'wa'), may hold values from -0.21875 to 0.21875
- value_proj2: bfloat16 [768, 768], P('ctx', 'wa'), may hold values from -0.21875 to 0.21875
- output_proj2: bfloat16 [768, 768], P('ctx', 'wa'), may hold values from -0.625 to 0.625
- expert_gain2: float32 [768], replicated, may hold values from 0.5 to 1.5
- router: float32 [768, 16], replicated, may hold values from -0.21875 to 0.21875
- expert_up: bfloat16 [16, 768, 3072], P('ctx', None, 'wa'), may hold values from -0.21875 to 0.21875
- expert_down: bfloat16 [16, 3072, 768], P('ctx', 'wa'), may hold values from -0.109375 to 0.109375
Outputs:
- result: bfloat16 [4096, 768], P('ctx')
- grad_tokens: float32 [4096, 768], P('ctx')
- grad_attend_gain1: float32 [768], replicated
- grad_rel_bias1: float32 [12, 32], P('wa')
- grad_query_proj1: float32 [768, 768], P('ctx', 'wa')
- grad_key_proj1: float32 [768, 768], P('ctx', 'wa')
- grad_value_proj1: float32 [768, 768], P('ctx', 'wa')
- grad_output_proj1: float32 [768, 768], P('ctx', 'wa')
- grad_dense_gain1: float32 [768], replicated
- grad_dense_up1: float32 [768, 3072], P('ctx', 'wa')
- grad_dense_down1: float32 [768, 3072], P('ctx', 'wa')
- grad_attend_gain2: float32 [768], replicated
- grad_rel_bias2: float32 [12, 32], P('wa')
- grad_query_proj2: float32 [768, 768], P('ctx', 'wa')
- grad_key_proj2: float32 [768, 768], P('ctx', 'wa')
- grad_value_proj2: float32 [768, 768], P('ctx', 'wa')
- grad_output_proj2: float32 [768, 768], P('ctx', 'wa')
- grad_expert_gain2: float32 [768], replicated
- grad_router: float32 [768, 16], replicated
- grad_expert_up: float32 [16, 768, 3072], P('ctx', None, 'wa')
- grad_expert_down: float32 [16, 3072, 768], P('ctx', 'wa')
The draws below stay inside these ranges and needn't reach their ends.
Inputs may be any that keep to these rules, and one draw needn't show every extreme that they name: `routes`: the 2 experts of a token differ. Among the 256 rows of one index of ctx no expert is named more than 64 times, a bound that some block reaches. `block_order`: each block position appears once.
All inputs are finite; a program needn't handle non-finite values.
Results may differ from the reference program's by a relative error of at most 0.029.
Values may be sent and summed in bfloat16 or wider, within the bound.
A program may use at most 448 MiB of HBM per device.

```python
import math
import jax
import jax.numpy as jnp
import numpy as np
from jax import lax

D = 768
H = 12
HS = 64
FF = 3072
NB = 32
TOP = 2
SEQS = 4
BLK = 64
HD = 768
EXPERTS = 16
TOK_DEV = 256
TOKENS = 4096
SEQ_LEN = 1024
CAP = 64
N_CTX = 16
N_WA = 2


def place_ends(values, rng, least, largest):
    shape = values.shape
    place = [jax.random.randint(jax.random.fold_in(rng, axis), (), 0, shape[axis]) for axis in range(len(shape))]
    values = values.at[tuple(place)].set(least)
    longest = shape.index(max(shape))
    place[longest] = (place[longest] + 1) % shape[longest]
    return values.at[tuple(place)].set(largest)


def steps_of(stream_key, extent, pieces, smallest, high):
    loudness, own = 1.0, jax.random.fold_in(stream_key, 6)
    for axis_at, shards_of in pieces:
        heights = jnp.exp(jax.random.uniform(jax.random.fold_in(own, axis_at), (shards_of,), jnp.float32, smallest / len(pieces), high / len(pieces)))
        loudness = loudness * jnp.repeat(heights, extent[axis_at] // shards_of).reshape([-1 if axis == axis_at else 1 for axis in range(len(extent))])
    return loudness


def routed_block(key, own, number, rows, amount, top, limit, lean):
    ranking = jax.random.permutation(key, amount)
    crowded, usual = portions_of(amount, rows * top, limit, lean, True), portions_of(amount, rows * top, limit, lean, False)
    places = jnp.arange(amount)

    def named(tallies, rotation):
        used = int((tallies > 0).sum())
        fixed = max(1, used // 4)
        moved = fixed + (places - fixed + rotation * (used - fixed)) % max(1, amount - fixed)
        return jnp.zeros((amount,), jnp.int32).at[ranking[jnp.where(places < fixed, places, moved)]].set(jnp.asarray(tallies, jnp.int32))

    tallies = jnp.where(number % 4 == 0, named(crowded, number // 4), named(usual, number - number // 4 - 1))
    mixed = jax.random.permutation(jax.random.fold_in(own, 3), amount)
    donor, receiver = mixed[0:amount // 2 * 2:2], mixed[1:amount // 2 * 2:2]
    room = jnp.minimum(tallies[donor] - 1, limit - tallies[receiver]) // 2
    room = jnp.where((donor == ranking[0]) | (receiver == ranking[0]) | (tallies[receiver] == 0), 0, jnp.maximum(room, 0))
    moved = jax.random.randint(jax.random.fold_in(own, 4), (amount // 2,), 0, 1 << 20) % (room + 1)
    tallies = tallies.at[donor].add(-moved).at[receiver].add(moved)
    items = jnp.searchsorted(jnp.cumsum(tallies), jnp.arange(rows * top), side="right").astype(jnp.int32)
    listing = items.reshape(top, rows).T
    listing = listing[jax.random.permutation(jax.random.fold_in(own, 1), rows)]
    rotation = jax.random.randint(jax.random.fold_in(own, 2), (rows, 1), 0, top)
    return jnp.take_along_axis(listing, (jnp.arange(top)[None, :] + rotation) % top, axis=1)


def portions_of(count, total, reach, lean, full):
    portions = [(1 << 20) // math.isqrt(rank ** lean) + 1 for rank in range(1, count + 1)]
    largest = reach if full else min(reach, max(-(-total // count), total * portions[0] // sum(portions)))
    least = 1 if total - largest >= count - 1 else 0
    holding, spare = [largest] + [least] * (count - 1), total - largest - least * (count - 1)
    while spare > 0:
        free = [i for i in range(1, count) if holding[i] < largest] or [i for i in range(1, count) if holding[i] < reach]
        whole, budget = sum([portions[i] for i in free]), spare
        for i in free:
            more = min(reach - holding[i], max(1, budget * portions[i] // whole), spare)
            holding[i] = holding[i] + more
            spare = spare - more
    return np.array(holding)


def normal_values(own_key, dims, scale, limit, cuts=(), kind=jnp.bfloat16):
    values = scale * jax.random.normal(own_key, dims, jnp.float32)
    if cuts:
        values = values * steps_of(own_key, dims, cuts, -0.22, 0.18)
    return jnp.clip(values, -limit, limit).astype(kind)


def setup_inputs(seed: int = 0) -> dict:
    key_list = jax.random.split(jax.random.key(seed), 25)
    tokens = normal_values(key_list[0], (TOKENS, D), 1.0, 6.0, ((0, 16),))
    cotangent = normal_values(key_list[1], (TOKENS, D), 1.0, 6.0, ((0, 16),))
    routes_keys = jax.random.split(jax.random.fold_in(key_list[2], 1), TOKENS // TOK_DEV)
    routes_turns = jax.random.permutation(jax.random.fold_in(key_list[2], 3), TOKENS // TOK_DEV)
    routes = jax.vmap(lambda own, number: routed_block(jax.random.fold_in(key_list[2], 2), own, number, TOK_DEV, EXPERTS, TOP, CAP, 1))(routes_keys, routes_turns).reshape((TOKENS, TOP))
    buckets = place_ends(jax.random.randint(key_list[3], (SEQ_LEN,), 0, NB), jax.random.fold_in(key_list[3], 1), 0, NB - 1).astype(jnp.int32)
    block_order = jax.random.permutation(key_list[4], N_CTX).astype(jnp.int32)
    attend_gain1 = jnp.clip(1.0 + 0.1 * jax.random.normal(key_list[5], (D,), jnp.float32), 0.5, 1.5)
    rel_bias1 = normal_values(key_list[6], (H, NB), 1.0, 4.0, ((0, 2),), jnp.float32)
    query_proj1 = normal_values(key_list[7], (D, HD), D ** -0.5, 0.21875, ((0, 16), (1, 2)))
    key_proj1 = normal_values(key_list[8], (D, HD), D ** -0.5, 0.21875, ((0, 16), (1, 2)))
    value_proj1 = normal_values(key_list[9], (D, HD), D ** -0.5, 0.21875, ((0, 16), (1, 2)))
    output_proj1 = normal_values(key_list[10], (D, HD), (HD // 8) ** -0.5, 0.625, ((0, 16), (1, 2)))
    dense_gain1 = jnp.clip(1.0 + 0.1 * jax.random.normal(key_list[11], (D,), jnp.float32), 0.5, 1.5)
    dense_up1 = normal_values(key_list[12], (D, FF), D ** -0.5, 0.21875, ((0, 16), (1, 2)))
    dense_down1 = normal_values(key_list[13], (D, FF), FF ** -0.5, 0.109375, ((0, 16), (1, 2)))
    attend_gain2 = jnp.clip(1.0 + 0.1 * jax.random.normal(key_list[14], (D,), jnp.float32), 0.5, 1.5)
    rel_bias2 = normal_values(key_list[15], (H, NB), 1.0, 4.0, ((0, 2),), jnp.float32)
    query_proj2 = normal_values(key_list[16], (D, HD), D ** -0.5, 0.21875, ((0, 16), (1, 2)))
    key_proj2 = normal_values(key_list[17], (D, HD), D ** -0.5, 0.21875, ((0, 16), (1, 2)))
    value_proj2 = normal_values(key_list[18], (D, HD), D ** -0.5, 0.21875, ((0, 16), (1, 2)))
    output_proj2 = normal_values(key_list[19], (D, HD), (HD // 8) ** -0.5, 0.625, ((0, 16), (1, 2)))
    expert_gain2 = jnp.clip(1.0 + 0.1 * jax.random.normal(key_list[20], (D,), jnp.float32), 0.5, 1.5)
    router = normal_values(key_list[21], (D, EXPERTS), D ** -0.5, 0.21875, (), jnp.float32)
    expert_up = normal_values(key_list[22], (EXPERTS, D, FF), D ** -0.5, 0.21875, ((0, 16), (2, 2)))
    expert_down = normal_values(key_list[23], (EXPERTS, FF, D), FF ** -0.5, 0.109375, ((0, 16), (1, 2)))
    return dict(tokens=tokens, cotangent=cotangent, routes=routes, buckets=buckets, block_order=block_order, attend_gain1=attend_gain1, rel_bias1=rel_bias1, query_proj1=query_proj1, key_proj1=key_proj1, value_proj1=value_proj1, output_proj1=output_proj1, dense_gain1=dense_gain1, dense_up1=dense_up1, dense_down1=dense_down1, attend_gain2=attend_gain2, rel_bias2=rel_bias2, query_proj2=query_proj2, key_proj2=key_proj2, value_proj2=value_proj2, output_proj2=output_proj2, expert_gain2=expert_gain2, router=router, expert_up=expert_up, expert_down=expert_down)


@jax.custom_vjp
def low(v):
    return lax.optimization_barrier(v.astype(jnp.bfloat16)).astype(jnp.float32)

@jax.custom_vjp
def low_back(v):
    return v

def low_keep(v):
    return (low(v), None)

def low_pass(kept, grad):
    return (grad,)

def back_keep(v):
    return (v, None)

def back_low(kept, grad):
    return (low(grad),)
low.defvjp(low_keep, low_pass)
low_back.defvjp(back_keep, back_low)
HIGHEST = lax.Precision.HIGHEST
epsilon = 1e-06
masked_value = -1e+30

def round_both(values):
    return low_back(low(values))

def gelu_fn(values):
    return jax.nn.gelu(values, approximate=True)

def rms_norm(inputs, gain):
    inv_rms = lax.rsqrt(lax.optimization_barrier(jnp.mean(inputs * inputs, axis=-1, keepdims=True)) + epsilon)
    return inputs * inv_rms * gain

def to_seq(values):
    return values.reshape(N_CTX, SEQS, BLK, values.shape[-1]).transpose(1, 0, 2, 3).reshape(SEQS, N_CTX * BLK, values.shape[-1])

def from_seq(values):
    return values.reshape(SEQS, N_CTX, BLK, values.shape[-1]).transpose(1, 0, 2, 3).reshape(N_CTX * SEQS * BLK, values.shape[-1])

def attention(normed_low, query_w, key_w, value_w, output_w, rel_bias, buckets, positions):
    block_rows = min(512, SEQ_LEN)
    queries = round_both(jnp.dot(normed_low, query_w, precision=HIGHEST))
    keys = round_both(jnp.dot(normed_low, key_w, precision=HIGHEST))
    values = round_both(jnp.dot(normed_low, value_w, precision=HIGHEST))
    query_seq = to_seq(queries).reshape(SEQS, SEQ_LEN // block_rows, block_rows, H, HS)
    key_seq = to_seq(keys).reshape(SEQS, SEQ_LEN, H, HS)
    value_seq = to_seq(values).reshape(SEQS, SEQ_LEN, H, HS)
    query_pos = positions.reshape(SEQ_LEN // block_rows, block_rows)

    def per_seq(seq_items):
        query_blocks, key_rows, value_rows = seq_items

        def per_block(block_items):
            query_block, block_pos = block_items
            distance = block_pos[:, None] - positions[None, :]
            pos_bias = rel_bias[:, buckets[jnp.maximum(distance, 0)]]
            scores = jnp.einsum('qhd,khd->hqk', query_block, key_rows, precision=HIGHEST) * 0.125 + pos_bias
            scores = low_back(jnp.where((distance >= 0)[None], scores, masked_value))
            attn_probs = jax.nn.softmax(scores, axis=-1)
            return jnp.einsum('hqk,khd->qhd', low(attn_probs), value_rows, precision=HIGHEST)
        return lax.map(jax.checkpoint(per_block), (query_blocks, query_pos))
    mixed = lax.map(per_seq, (query_seq, key_seq, value_seq))
    mixed = round_both(from_seq(mixed.reshape(SEQS, SEQ_LEN, H * HS)))
    return low_back(jnp.einsum('te,de->td', mixed, output_w, precision=HIGHEST))

def experts(normed, router, expert_up, expert_down, routes, token_of, filled, slot_place):
    logits = jnp.dot(normed, router, precision=HIGHEST)
    gate_probs = jax.nn.softmax(jnp.take_along_axis(logits, routes, axis=1), axis=-1)
    inputs = low(normed)[token_of] * filled[..., None]

    def per_expert(expert_items):
        expert_rows, up_weight, down_weight = expert_items
        pre_act = low_back(jnp.dot(expert_rows, up_weight, precision=HIGHEST))
        hidden = low(gelu_fn(pre_act)).reshape(-1, N_WA, FF // N_WA)
        half_parts = jnp.einsum('cwf,wfd->wcd', hidden, down_weight.reshape(N_WA, FF // N_WA, D), precision=HIGHEST)
        return lax.optimization_barrier(jnp.sum(round_both(half_parts), axis=0))
    results = lax.map(jax.checkpoint(per_expert), (inputs, expert_up, expert_down))
    picked = results.reshape(-1, D)[slot_place].reshape(TOKENS, TOP, D)
    return lax.optimization_barrier(jnp.sum(gate_probs[..., None] * picked, axis=1))

def reference(tokens, cotangent, routes, buckets, block_order, attend_gain1, rel_bias1, query_proj1, key_proj1, value_proj1, output_proj1, dense_gain1, dense_up1, dense_down1, attend_gain2, rel_bias2, query_proj2, key_proj2, value_proj2, output_proj2, expert_gain2, router, expert_up, expert_down):
    positions = (block_order[:, None] * BLK + jnp.arange(BLK, dtype=jnp.int32)[None, :]).reshape(-1).astype(jnp.int32)
    flat_routes = routes.reshape(N_CTX, TOK_DEV * TOP)
    onehot = (flat_routes[..., None] == jnp.arange(EXPERTS, dtype=jnp.int32)[None, None, :]).astype(jnp.int32)
    slot_rank = lax.optimization_barrier(jnp.sum((jnp.cumsum(onehot, axis=1) - onehot) * onehot, axis=-1))
    source = jnp.broadcast_to(jnp.arange(N_CTX, dtype=jnp.int32)[:, None], flat_routes.shape)
    slot_place = (flat_routes * (N_CTX * CAP) + source * CAP + slot_rank).reshape(-1).astype(jnp.int32)
    token_ids = (jnp.arange(TOKENS * TOP, dtype=jnp.int32) // TOP).astype(jnp.int32)
    token_of = jnp.zeros((EXPERTS * N_CTX * CAP,), jnp.int32).at[slot_place].set(token_ids).reshape(EXPERTS, N_CTX * CAP)
    filled = jnp.zeros((EXPERTS * N_CTX * CAP,), jnp.float32).at[slot_place].set(1.0).reshape(EXPERTS, N_CTX * CAP)

    def forward(tokens_f, gain_a1, rel_one, query_one, key_one, value_one, output_one, gain_d1, up_one, down_one, gain_a2, rel_two, query_two, key_two, value_two, output_two, gain_e2, router_w, up_experts, down_experts):
        normed = rms_norm(tokens_f, gain_a1)
        after_attn1 = tokens_f + attention(low(normed), query_one, key_one, value_one, output_one, rel_one, buckets, positions)
        normed = rms_norm(after_attn1, gain_d1)
        pre_act = low_back(jnp.dot(low(normed), up_one, precision=HIGHEST))
        hidden = low(gelu_fn(pre_act))
        after_dense1 = after_attn1 + low_back(jnp.einsum('tf,df->td', hidden, down_one, precision=HIGHEST))
        normed = rms_norm(after_dense1, gain_a2)
        after_attn2 = after_dense1 + attention(low(normed), query_two, key_two, value_two, output_two, rel_two, buckets, positions)
        normed = rms_norm(after_attn2, gain_e2)
        return after_attn2 + experts(normed, router_w, up_experts, down_experts, routes, token_of, filled, slot_place)
    primals = (tokens.astype(jnp.float32), attend_gain1.astype(jnp.float32), rel_bias1.astype(jnp.float32), query_proj1.astype(jnp.float32), key_proj1.astype(jnp.float32), value_proj1.astype(jnp.float32), output_proj1.astype(jnp.float32), dense_gain1.astype(jnp.float32), dense_up1.astype(jnp.float32), dense_down1.astype(jnp.float32), attend_gain2.astype(jnp.float32), rel_bias2.astype(jnp.float32), query_proj2.astype(jnp.float32), key_proj2.astype(jnp.float32), value_proj2.astype(jnp.float32), output_proj2.astype(jnp.float32), expert_gain2.astype(jnp.float32), router.astype(jnp.float32), expert_up.astype(jnp.float32), expert_down.astype(jnp.float32))
    result, pull_back = jax.vjp(forward, *primals)
    all_grads = pull_back(cotangent.astype(jnp.float32))
    return (result.astype(jnp.bfloat16), all_grads[0], all_grads[1], all_grads[2], all_grads[3], all_grads[4], all_grads[5], all_grads[6], all_grads[7], all_grads[8], all_grads[9], all_grads[10], all_grads[11], all_grads[12], all_grads[13], all_grads[14], all_grads[15], all_grads[16], all_grads[17], all_grads[18], all_grads[19])
```

```python
import jax
import jax.numpy as jnp
from jax import lax
from jax.experimental import pallas as pl
from jax.experimental.pallas import tpu as pltpu
from jax.sharding import PartitionSpec as P

HS = 64
SEQS = 4
BLK = 64
TILE = 256
PER = TILE // BLK


HIGHEST = lax.Precision.HIGHEST
epsilon = 1e-06
masked_value = -1e30


def gelu_fn(values):
    return jax.nn.gelu(values, approximate=True)


def rms_norm(inputs, gain):
    inv_rms = lax.rsqrt(jnp.mean(inputs * inputs, axis=-1, keepdims=True) + epsilon)
    return (inputs * inv_rms * gain, inv_rms)


def norm_back(inputs, inv_rms, gain, grad_normed):
    weighted = grad_normed * gain
    gain_grad = jnp.sum(grad_normed * inputs * inv_rms, axis=0)
    grad_inputs = inv_rms * weighted - inputs * inv_rms * inv_rms * inv_rms * jnp.mean(
        weighted * inputs, axis=-1, keepdims=True
    )
    return (grad_inputs, gain_grad)


def other_core(values):
    return lax.ppermute(values, "wa", [(0, 1), (1, 0)])


def half_total(partial_value):
    own = partial_value.astype(jnp.bfloat16)
    return own.astype(jnp.float32) + other_core(own).astype(jnp.float32)


def to_parts(values):
    return lax.all_to_all(values, "ctx", 0, 0, tiled=True)


def bucket_hot(rel_local, buckets):
    bucket_count = rel_local.shape[1]
    return (buckets[:, None] == jnp.arange(bucket_count, dtype=jnp.int32)[None, :]).astype(
        jnp.float32
    )


def bias_strips(rel_local, hot, group):
    seq_len = hot.shape[0]
    heads = rel_local.shape[0] // 2
    by_distance = jnp.dot(rel_local, hot.T, precision=HIGHEST)
    by_distance = lax.dynamic_slice_in_dim(by_distance, group * heads, heads, 0)
    ext = jnp.concatenate([jnp.full((heads, TILE), masked_value, jnp.float32), by_distance], 1)
    ext = ext[:, ::-1]
    total = ext.shape[1]
    rows = []
    for diag in range(seq_len // TILE):
        start = total - (diag + 2) * TILE
        strip = ext[:, start : start + 2 * TILE]
        rows.append(jnp.stack([jnp.roll(strip, i, axis=1) for i in range(8)], axis=1))
    return jnp.stack(rows, axis=1)


def bias_grad(skewed, hot, group, head_count):
    heads, diags = skewed.shape[:2]
    seq_len, bucket_count = hot.shape
    sums = sum(jnp.roll(skewed[:, :, i], -i, axis=-1) for i in range(8))
    padded = jnp.concatenate(
        [jnp.zeros((TILE, bucket_count), jnp.float32), hot, jnp.zeros((1, bucket_count), jnp.float32)]
    )[::-1]
    total = padded.shape[0]
    windows = []
    for diag in range(diags):
        low_at = total - 1 - (diag * TILE + TILE)
        high_at = total - 1 - (diag * TILE + 2 * TILE)
        windows.append(padded[low_at : low_at + TILE])
        windows.append(padded[high_at : high_at + TILE])
    spread = jnp.concatenate(windows, axis=0)
    own = jnp.dot(sums.reshape(heads, -1), spread, precision=HIGHEST)
    whole = jnp.zeros((head_count, bucket_count), jnp.float32)
    return lax.dynamic_update_slice_in_dim(whole, own, group * heads, 0)


def fill_bias(strips_ref, bias, head):
    for diag in range(bias.shape[0]):
        strip = strips_ref[head, diag]
        for a in range(TILE // 8):
            shift = (2 * TILE - (TILE - 1 - 8 * a)) % (2 * TILE)
            bias[diag, 8 * a : 8 * a + 8, :] = pltpu.roll(strip, shift, 1)[:, :TILE]


def sort_blocks(where_ref, arrived_ref, held, count):
    parts = held.shape[0]

    @pl.loop(0, count)
    def _(b):
        block = arrived_ref[where_ref[b]]
        for part in range(parts):
            held[part, pl.ds(pl.multiple_of(b * BLK, BLK), BLK), :] = block[
                :, part * HS : (part + 1) * HS
            ]


def rows_of(tile):
    return pl.ds(pl.multiple_of(tile * TILE, TILE), TILE)


def dot_nt(a, b):
    return lax.dot_general(a, b, (((1,), (1,)), ((), ())), preferred_element_type=jnp.float32)


def dot_tn(a, b):
    return lax.dot_general(a, b, (((0,), (0,)), ((), ())), preferred_element_type=jnp.float32)


def forward_kernel(where_ref, arrived_ref, strips_ref, send_ref, mixed_ref, log_ref, held, bias):
    count = arrived_ref.shape[0]
    heads = strips_ref.shape[0]
    tiles = count // PER
    share = where_ref[count]
    sort_blocks(where_ref, arrived_ref, held, count)
    send_ref[...] = jnp.zeros_like(send_ref)

    @pl.loop(0, heads)
    def _(head):
        fill_bias(strips_ref, bias, head)
        for turn in range(2):
            tile = share if turn == 0 else tiles - 1 - share
            query = held[head, rows_of(tile), :]

            def step(j, carry):
                top, total, acc = carry
                key = held[heads + head, rows_of(j), :]
                value = held[2 * heads + head, rows_of(j), :]
                scores = dot_nt(query, key) * 0.125 + bias[tile - j]
                new_top = jnp.maximum(top, jnp.max(scores, axis=1, keepdims=True))
                expo = jnp.exp(scores - new_top)
                keep = jnp.exp(top - new_top)
                total = total * keep + jnp.sum(expo, axis=1, keepdims=True)
                acc = acc * keep + jnp.dot(
                    expo.astype(jnp.bfloat16), value, preferred_element_type=jnp.float32
                )
                return new_top, total, acc

            top, total, acc = lax.fori_loop(
                0,
                tile + 1,
                step,
                (
                    jnp.full((TILE, 1), masked_value, jnp.float32),
                    jnp.zeros((TILE, 1), jnp.float32),
                    jnp.zeros((TILE, HS), jnp.float32),
                ),
            )
            mixed_ref[head, turn * TILE : (turn + 1) * TILE, :] = acc / total
            log_ref[head, turn * TILE : (turn + 1) * TILE, :] = top + jnp.log(total)

    for turn in range(2):
        tile = share if turn == 0 else tiles - 1 - share
        for i in range(PER):
            at = turn * TILE + i * BLK
            block = jnp.concatenate([mixed_ref[h, at : at + BLK, :] for h in range(heads)], axis=1)
            send_ref[where_ref[tile * PER + i]] = block.astype(jnp.bfloat16)


def backward_kernel(
    where_ref,
    arrived_ref,
    strips_ref,
    grad_ref,
    mixed_ref,
    log_ref,
    send_ref,
    skew_ref,
    held,
    grads,
    sums,
    bias,
    score_sum,
):
    count = arrived_ref.shape[0]
    heads = strips_ref.shape[0]
    tiles = count // PER
    share = where_ref[count]
    sort_blocks(where_ref, arrived_ref, held, count)
    sort_blocks(where_ref, grad_ref, grads, count)
    sums[...] = jnp.zeros_like(sums)

    @pl.loop(0, heads)
    def _(head):
        fill_bias(strips_ref, bias, head)
        score_sum[...] = jnp.zeros_like(score_sum)
        for turn in range(2):
            tile = share if turn == 0 else tiles - 1 - share
            query = held[head, rows_of(tile), :]
            grad = grads[head, rows_of(tile), :]
            log_total = log_ref[head, turn * TILE : (turn + 1) * TILE, :]
            mixed = mixed_ref[head, turn * TILE : (turn + 1) * TILE, :]
            delta = jnp.sum(grad.astype(jnp.float32) * mixed, axis=1, keepdims=True)

            @pl.loop(0, tile + 1)
            def _(j):
                key = held[heads + head, rows_of(j), :]
                value = held[2 * heads + head, rows_of(j), :]
                scores = dot_nt(query, key) * 0.125 + bias[tile - j]
                probs = jnp.exp(scores - log_total)
                grad_scores = (probs * (dot_nt(grad, value) - delta)).astype(jnp.bfloat16)
                score_sum[tile - j] += grad_scores.astype(jnp.float32)
                sums[head, rows_of(tile), :] += jnp.dot(
                    grad_scores, key, preferred_element_type=jnp.float32
                )
                sums[heads + head, rows_of(j), :] += dot_tn(grad_scores, query)
                sums[2 * heads + head, rows_of(j), :] += dot_tn(probs.astype(jnp.bfloat16), grad)

        for diag in range(tiles):
            total = jnp.zeros((8, 2 * TILE), jnp.float32)
            for a in range(TILE // 8):
                rows = jnp.concatenate(
                    [score_sum[diag, 8 * a : 8 * a + 8, :], jnp.zeros((8, TILE), jnp.float32)],
                    axis=1,
                )
                total = total + pltpu.roll(rows, (2 * TILE - 8 * a) % (2 * TILE), 1)
            skew_ref[head, diag] = total

    @pl.loop(0, count)
    def _(b):
        at = pl.ds(pl.multiple_of(b * BLK, BLK), BLK)
        parts = [
            sums[part, at, :] * (0.125 if part < 2 * heads else 1.0) for part in range(3 * heads)
        ]
        send_ref[where_ref[b]] = jnp.concatenate(parts, axis=1).astype(jnp.bfloat16)


def kernel_call(body, where, inputs, outs, scratch, cost):
    return pl.pallas_call(
        body,
        in_specs=[pl.BlockSpec(memory_space=pltpu.SMEM)]
        + [pl.BlockSpec(memory_space=pltpu.VMEM)] * len(inputs),
        out_specs=[pl.BlockSpec(memory_space=pltpu.VMEM)] * len(outs),
        out_shape=outs,
        scratch_shapes=scratch,
        compiler_params=pltpu.CompilerParams(vmem_limit_bytes=56 * 1024 * 1024),
        cost_estimate=pl.CostEstimate(flops=cost, bytes_accessed=4000000, transcendentals=1000000),
    )(where, *inputs)


def attention_forward(normed_low, gathered, strips, where):
    width = gathered.shape[1] // 4
    heads = width // HS // 2
    count = lax.axis_size("ctx")
    split = count // SEQS // 2
    cols = heads * HS
    tiles = count // PER
    projected = jnp.dot(
        normed_low, gathered[:, : 3 * width], preferred_element_type=jnp.float32
    ).astype(jnp.bfloat16)
    groups = []
    for g in range(2):
        groups.append(
            jnp.concatenate(
                [
                    projected[:, p * width + g * cols : p * width + (g + 1) * cols]
                    for p in range(3)
                ],
                axis=1,
            ).reshape(SEQS, BLK, 3 * cols)
        )
    outgoing = jnp.broadcast_to(
        jnp.stack(groups, axis=1)[:, :, None], (SEQS, 2, split, BLK, 3 * cols)
    ).reshape(count, BLK, 3 * cols)
    arrived = to_parts(outgoing)
    send, mixed, log_total = kernel_call(
        forward_kernel,
        where,
        (arrived, strips),
        [
            jax.ShapeDtypeStruct((count, BLK, cols), jnp.bfloat16),
            jax.ShapeDtypeStruct((heads, 2 * TILE, HS), jnp.float32),
            jax.ShapeDtypeStruct((heads, 2 * TILE, 1), jnp.float32),
        ],
        [
            pltpu.VMEM((3 * heads, count * BLK, HS), jnp.bfloat16),
            pltpu.VMEM((tiles, TILE, TILE), jnp.float32),
        ],
        heads * (tiles + 1) * TILE * TILE * HS * 4,
    )
    mixed_low = from_parts(send, split).reshape(SEQS, 2, BLK, cols)
    mixed_low = mixed_low.transpose(0, 2, 1, 3).reshape(SEQS * BLK, width)
    branch = half_total(
        lax.dot_general(
            mixed_low,
            gathered[:, 3 * width :],
            (((1,), (1,)), ((), ())),
            preferred_element_type=jnp.float32,
        )
    )
    return (branch, (arrived, mixed, log_total, mixed_low))


def from_parts(send, split):
    parts = to_parts(send)
    count, rows, cols = parts.shape
    parts = parts.reshape(count // split, split, rows, cols)
    return jnp.sum(parts.astype(jnp.float32), axis=1).astype(jnp.bfloat16)


def attention_backward(grad_branch, normed_low, gathered, kept_fwd, strips, where):
    arrived, mixed, log_total, mixed_low = kept_fwd
    width = gathered.shape[1] // 4
    heads = width // HS // 2
    count = lax.axis_size("ctx")
    split = count // SEQS // 2
    cols = heads * HS
    tiles = count // PER
    grad_low = grad_branch.astype(jnp.bfloat16)
    grad_mixed = jnp.dot(
        grad_low, gathered[:, 3 * width :], preferred_element_type=jnp.float32
    ).astype(jnp.bfloat16)
    outgoing = grad_mixed.reshape(SEQS, BLK, 2, cols).transpose(0, 2, 1, 3)
    outgoing = jnp.broadcast_to(
        outgoing[:, :, None], (SEQS, 2, split, BLK, cols)
    ).reshape(count, BLK, cols)
    grad_arrived = to_parts(outgoing)
    output_grad = jnp.einsum("td,te->de", grad_low, mixed_low, preferred_element_type=jnp.float32)
    send, skewed = kernel_call(
        backward_kernel,
        where,
        (arrived, strips, grad_arrived, mixed, log_total),
        [
            jax.ShapeDtypeStruct((count, BLK, 3 * cols), jnp.bfloat16),
            jax.ShapeDtypeStruct((heads, tiles, 8, 2 * TILE), jnp.float32),
        ],
        [
            pltpu.VMEM((3 * heads, count * BLK, HS), jnp.bfloat16),
            pltpu.VMEM((heads, count * BLK, HS), jnp.bfloat16),
            pltpu.VMEM((3 * heads, count * BLK, HS), jnp.float32),
            pltpu.VMEM((tiles, TILE, TILE), jnp.float32),
            pltpu.VMEM((tiles, TILE, TILE), jnp.float32),
        ],
        heads * (tiles + 1) * TILE * TILE * HS * 10,
    )
    back = from_parts(send, split).reshape(SEQS, 2, BLK, 3, cols)
    back = back.transpose(0, 2, 3, 1, 4).reshape(SEQS * BLK, 3 * width)
    grad_partial = lax.dot_general(
        back,
        gathered[:, : 3 * width],
        (((1,), (1,)), ((), ())),
        preferred_element_type=jnp.float32,
    )
    weight_grad = jnp.einsum("td,te->de", normed_low, back, preferred_element_type=jnp.float32)
    weight_grads = jnp.concatenate(
        [weight_grad.astype(jnp.bfloat16), output_grad.astype(jnp.bfloat16)], axis=1
    )
    return (half_total(grad_partial), weight_grads, skewed)


def sum_at_owner(array):
    return lax.psum_scatter(array, "ctx", scatter_dimension=0, tiled=True).astype(jnp.float32)


def dot_back(a, b):
    return lax.dot_general(a, b, (((1,), (1,)), ((), ())), preferred_element_type=jnp.float32)


def gelu_back(pre_act, grad_hidden):
    _, gelu_pull = jax.vjp(gelu_fn, pre_act)
    return gelu_pull(grad_hidden)[0].astype(jnp.bfloat16)


def expert_block(normed, routes, router, expert_up, expert_down, grad_out):
    normed_low = normed.astype(jnp.bfloat16)
    tok_rows, top_count = routes.shape
    num_experts = router.shape[1]
    width = normed.shape[1]
    capacity = 2 * tok_rows * top_count // num_experts
    half = capacity // 2
    expert_up = expert_up[0]
    expert_down = expert_down[0]
    expert_ids = jnp.arange(num_experts, dtype=jnp.int32)
    flat_routes = routes.reshape(-1)
    items = flat_routes.shape[0]
    one_hot = flat_routes[:, None] == expert_ids[None, :]
    order = jnp.arange(items, dtype=jnp.int32)
    earlier = (order[:, None] > order[None, :]).astype(jnp.bfloat16)
    ranks = jnp.dot(earlier, one_hot.astype(jnp.bfloat16), preferred_element_type=jnp.float32)
    slot_rank = jnp.sum(jnp.where(one_hot, ranks, 0.0), axis=1).astype(jnp.int32)
    rank_here = slot_rank - half * lax.axis_index("wa")
    inside = (rank_here >= 0) & (rank_here < half)
    place = jnp.where(inside, flat_routes * half + rank_here, -1)
    slots = num_experts * half
    pick = (place[:, None] == jnp.arange(slots, dtype=jnp.int32)[None, :]).astype(jnp.bfloat16)
    logits = jnp.dot(normed, router, precision=HIGHEST)
    route_hot = (routes[..., None] == expert_ids[None, None, :]).astype(jnp.float32)
    chosen_logits = jnp.sum(logits[:, None, :] * route_hot, axis=-1)
    gate_probs = jax.nn.softmax(chosen_logits, axis=-1)
    grad_choice = (gate_probs[..., None] * grad_out[:, None, :]).astype(jnp.bfloat16)
    both = jnp.concatenate(
        [jnp.repeat(normed_low, top_count, axis=0), grad_choice.reshape(items, width)], axis=1
    )
    outgoing = lax.dot_general(
        pick, both, (((0,), (0,)), ((), ())), preferred_element_type=jnp.float32
    ).astype(jnp.bfloat16)
    here = to_parts(outgoing.reshape(num_experts, half, 2 * width)).reshape(slots, 2 * width)
    rows = jnp.concatenate([here, other_core(here)], axis=0)
    inputs = rows[:, :width]
    grad_rows = rows[:, width:]
    pre_act = jnp.dot(inputs, expert_up, preferred_element_type=jnp.float32)
    hidden = gelu_fn(pre_act).astype(jnp.bfloat16)
    part = jnp.dot(hidden, expert_down, preferred_element_type=jnp.float32).astype(jnp.bfloat16)
    grad_pre = gelu_back(pre_act, dot_back(grad_rows, expert_down))
    grad_part = dot_back(grad_pre, expert_up).astype(jnp.bfloat16)
    parts = jnp.concatenate([part, grad_part], axis=1)
    totals = (
        parts[:slots].astype(jnp.float32) + other_core(parts[slots:]).astype(jnp.float32)
    ).astype(jnp.bfloat16)
    back = to_parts(totals.reshape(num_experts, half, 2 * width)).reshape(slots, 2 * width)
    down_grad = jnp.einsum("cf,cd->fd", hidden, grad_rows, preferred_element_type=jnp.float32)
    up_grad = jnp.einsum("cd,cf->df", inputs, grad_pre, preferred_element_type=jnp.float32)
    chosen = jnp.dot(pick, back[:, :width], preferred_element_type=jnp.float32)
    pick_token = jnp.sum(
        pick.astype(jnp.float32).reshape(tok_rows, top_count, slots), axis=1
    ).astype(jnp.bfloat16)
    grad_token = jnp.dot(pick_token, back[:, width:], preferred_element_type=jnp.float32)
    joined = half_total(jnp.concatenate([chosen, grad_token], axis=0))
    per_choice = joined[:items].reshape(tok_rows, top_count, width)
    mixture = jnp.sum(gate_probs[..., None] * per_choice, axis=1)
    grad_gate = jnp.sum(grad_out[:, None, :] * per_choice, axis=-1)
    grad_chosen = gate_probs * (grad_gate - jnp.sum(gate_probs * grad_gate, axis=-1, keepdims=True))
    grad_logits = jnp.sum(grad_chosen[..., None] * route_hot, axis=1)
    router_grad = jnp.dot(normed.T, grad_logits, precision=HIGHEST)
    grad_from_router = jnp.dot(grad_logits, router.T, precision=HIGHEST)
    grad_normed = joined[items:] + grad_from_router
    return (mixture, grad_normed, router_grad, up_grad[None], down_grad[None])


def sum_everywhere(arrays):
    flat = jnp.concatenate([a.reshape(-1) for a in arrays])
    flat = lax.psum(flat, "ctx")
    out, at = ([], 0)
    for a in arrays:
        out.append(flat[at : at + a.size].reshape(a.shape))
        at += a.size
    return out


def local(
    tokens,
    cotangent,
    routes,
    buckets,
    block_order,
    attend_gain1,
    rel_bias1,
    query_proj1,
    key_proj1,
    value_proj1,
    output_proj1,
    dense_gain1,
    dense_up1,
    dense_down1,
    attend_gain2,
    rel_bias2,
    query_proj2,
    key_proj2,
    value_proj2,
    output_proj2,
    expert_gain2,
    router,
    expert_up,
    expert_down,
):
    count = lax.axis_size("ctx")
    split = count // SEQS // 2
    here = lax.axis_index("ctx")
    group = (here // split) % 2
    ids = jnp.arange(count, dtype=jnp.int32)
    place_of = jnp.sum(jnp.where(block_order[:, None] == ids[None, :], ids[:, None], 0), axis=0)
    where = jnp.concatenate([place_of, (here % split)[None].astype(jnp.int32)])
    head_count = rel_bias1.shape[0]
    width = query_proj1.shape[1]
    gathered_one = lax.all_gather(
        jnp.concatenate([query_proj1, key_proj1, value_proj1, output_proj1], axis=1),
        "ctx",
        axis=0,
        tiled=True,
    )
    dense_full = lax.all_gather(
        jnp.concatenate([dense_up1, dense_down1], axis=1), "ctx", axis=0, tiled=True
    )
    gathered_two = lax.all_gather(
        jnp.concatenate([query_proj2, key_proj2, value_proj2, output_proj2], axis=1),
        "ctx",
        axis=0,
        tiled=True,
    )
    hidden_width = dense_up1.shape[1]
    up_full = dense_full[:, :hidden_width]
    down_full = dense_full[:, hidden_width:]
    hot = bucket_hot(rel_bias1, buckets)
    strips_one = bias_strips(rel_bias1, hot, group)
    strips_two = bias_strips(rel_bias2, hot, group)
    residual = tokens.astype(jnp.float32)
    normed_a1, inv_a1 = rms_norm(residual, attend_gain1)
    low_a1 = normed_a1.astype(jnp.bfloat16)
    branch_a1, kept_a1 = attention_forward(low_a1, gathered_one, strips_one, where)
    after_attn1 = residual + branch_a1
    normed_d1, inv_d1 = rms_norm(after_attn1, dense_gain1)
    low_d1 = normed_d1.astype(jnp.bfloat16)
    pre_d1 = jnp.dot(low_d1, up_full, preferred_element_type=jnp.float32)
    hidden_d1 = gelu_fn(pre_d1).astype(jnp.bfloat16)
    after_dense1 = after_attn1 + half_total(dot_back(hidden_d1, down_full))
    normed_a2, inv_a2 = rms_norm(after_dense1, attend_gain2)
    low_a2 = normed_a2.astype(jnp.bfloat16)
    branch_a2, kept_a2 = attention_forward(low_a2, gathered_two, strips_two, where)
    after_attn2 = after_dense1 + branch_a2
    normed_e2, inv_e2 = rms_norm(after_attn2, expert_gain2)
    grad_out = cotangent.astype(jnp.float32)
    mixture, grad_normed_e2, router_grad, up_grad, down_grad = expert_block(
        normed_e2, routes, router, expert_up, expert_down, grad_out
    )
    result = (after_attn2 + mixture).astype(jnp.bfloat16)
    grad_part, gain_e2 = norm_back(after_attn2, inv_e2, expert_gain2, grad_normed_e2)
    grad_residual = grad_out + grad_part
    grad_normed_a2, grads_two, skewed_two = attention_backward(
        grad_residual, low_a2, gathered_two, kept_a2, strips_two, where
    )
    own_two = sum_at_owner(grads_two)
    grad_part, gain_a2 = norm_back(after_dense1, inv_a2, attend_gain2, grad_normed_a2)
    grad_residual = grad_residual + grad_part
    grad_low = grad_residual.astype(jnp.bfloat16)
    down_part = jnp.einsum("td,tf->df", grad_low, hidden_d1, preferred_element_type=jnp.float32)
    grad_hidden = jnp.dot(grad_low, down_full, preferred_element_type=jnp.float32)
    grad_pre = gelu_back(pre_d1, grad_hidden)
    up_part = jnp.einsum("td,tf->df", low_d1, grad_pre, preferred_element_type=jnp.float32)
    grad_normed_d1 = half_total(dot_back(grad_pre, up_full))
    own_dense = sum_at_owner(
        jnp.concatenate([up_part.astype(jnp.bfloat16), down_part.astype(jnp.bfloat16)], axis=1)
    )
    grad_part, gain_d1 = norm_back(after_attn1, inv_d1, dense_gain1, grad_normed_d1)
    grad_residual = grad_residual + grad_part
    rel_two = bias_grad(skewed_two, hot, group, head_count)
    gain_d1, gain_a2, gain_e2, rel_two, router_grad = sum_everywhere(
        [gain_d1, gain_a2, gain_e2, rel_two, router_grad]
    )
    grad_normed_a1, grads_one, skewed_one = attention_backward(
        grad_residual, low_a1, gathered_one, kept_a1, strips_one, where
    )
    own_one = sum_at_owner(grads_one)
    grad_part, gain_a1 = norm_back(residual, inv_a1, attend_gain1, grad_normed_a1)
    grad_tokens = grad_residual + grad_part
    rel_one = bias_grad(skewed_one, hot, group, head_count)
    gain_a1, rel_one = sum_everywhere([gain_a1, rel_one])
    query_one, key_one, value_one, output_one = jnp.split(own_one, 4, axis=1)
    query_two, key_two, value_two, output_two = jnp.split(own_two, 4, axis=1)
    return (
        result,
        grad_tokens,
        gain_a1,
        rel_one,
        query_one,
        key_one,
        value_one,
        output_one,
        gain_d1,
        own_dense[:, :hidden_width],
        own_dense[:, hidden_width:],
        gain_a2,
        rel_two,
        query_two,
        key_two,
        value_two,
        output_two,
        gain_e2,
        router_grad,
        up_grad,
        down_grad,
    )


def solution(mesh):
    placed = (
        P("ctx", None),
        P("ctx", None),
        P("ctx", None),
        P(),
        P(),
        P(),
        P("wa", None),
        P("ctx", "wa"),
        P("ctx", "wa"),
        P("ctx", "wa"),
        P("ctx", "wa"),
        P(),
        P("ctx", "wa"),
        P("ctx", "wa"),
        P(),
        P("wa", None),
        P("ctx", "wa"),
        P("ctx", "wa"),
        P("ctx", "wa"),
        P("ctx", "wa"),
        P(),
        P(),
        P("ctx", None, "wa"),
        P("ctx", "wa", None),
    )
    return jax.shard_map(
        local,
        mesh=mesh,
        in_specs=placed,
        out_specs=(
            P("ctx", None),
            P("ctx", None),
            P(),
            P("wa", None),
            P("ctx", "wa"),
            P("ctx", "wa"),
            P("ctx", "wa"),
            P("ctx", "wa"),
            P(),
            P("ctx", "wa"),
            P("ctx", "wa"),
            P(),
            P("wa", None),
            P("ctx", "wa"),
            P("ctx", "wa"),
            P("ctx", "wa"),
            P("ctx", "wa"),
            P(),
            P(),
            P("ctx", None, "wa"),
            P("ctx", "wa", None),
        ),
        check_vma=False,
    )
```
